1024 devices in a mesh: dp: 16 (over x, z_hi, core), tensor: 64 (over z_lo, y).
Axes of the slice: x: 4, y: 4, z: 32 (z_hi: 2, z_lo: 16; z = z_hi * 16 + z_lo), core: 2. Of those that a mesh axis runs over, the one named last changes fastest.
Arguments:
- tokens: bfloat16 [2048, 2560], P(('dp', 'tensor')), may hold values from -6 to 6
- cotangent: bfloat16 [2048, 2560], P(('dp', 'tensor')), may hold values from -6 to 6
- gate_weight: bfloat16 [2560, 12800], P('dp', 'tensor'), may hold values from -0.125 to 0.125
- up_weight: bfloat16 [2560, 12800], P('dp', 'tensor'), may hold values from -0.125 to 0.125
- down_weight: bfloat16 [12800, 2560], P('tensor', 'dp'), may hold values from -0.0546875 to 0.0546875
Outputs:
- input_grad: bfloat16 [2048, 2560], P(('dp', 'tensor'))
- grad_gate: bfloat16 [2560, 12800], P('dp', 'tensor')
- grad_up: bfloat16 [2560, 12800], P('dp', 'tensor')
- grad_down: bfloat16 [12800, 2560], P('tensor', 'dp')
The draws below stay inside these ranges and needn't reach their ends.
All inputs are finite; a program needn't handle non-finite values.
Results may differ from the reference program's by a relative error of at most 0.017.
Values may be sent and summed in bfloat16 or wider, within the bound.
A program may use at most 64 MiB of HBM per device.

```python
import jax
import jax.numpy as jnp
from jax import lax

D = 2560
FF = 12800
GROUP = 128
TOKENS = 2048
N_DP = 16


def shard_levels(key, shape, cuts, least, high):
    factor_of, own = 1.0, jax.random.fold_in(key, 6)
    for position, blocks in cuts:
        draws = jnp.exp(jax.random.uniform(jax.random.fold_in(own, position), (blocks,), jnp.float32, least / len(cuts), high / len(cuts)))
        factor_of = factor_of * jnp.repeat(draws, shape[position] // blocks).reshape([-1 if axis == position else 1 for axis in range(len(shape))])
    return factor_of


def centred(key, shape, deviation, limit, shards=(), dtype=jnp.bfloat16):
    entries = deviation * jax.random.normal(key, shape, jnp.float32)
    if shards:
        entries = entries * shard_levels(key, shape, shards, -0.22, 0.18)
    return jnp.clip(entries, -limit, limit).astype(dtype)


def setup_inputs(seed: int = 0) -> dict:
    key_list = jax.random.split(jax.random.key(seed), 6)
    tokens = centred(key_list[0], (TOKENS, D), 1.0, 6.0, ((0, 1024),))
    cotangent = centred(key_list[1], (TOKENS, D), 1.0, 6.0, ((0, 1024),))
    gate_weight = centred(key_list[2], (D, FF), D ** -0.5, 0.125, ((0, 16), (1, 64)))
    up_weight = centred(key_list[3], (D, FF), D ** -0.5, 0.125, ((0, 16), (1, 64)))
    down_weight = centred(key_list[4], (FF, D), FF ** -0.5, 0.0546875, ((0, 64), (1, 16)))
    return dict(tokens=tokens, cotangent=cotangent, gate_weight=gate_weight, up_weight=up_weight, down_weight=down_weight)


def reference(tokens, cotangent, gate_weight, up_weight, down_weight):
    gate = jnp.dot(tokens, gate_weight, preferred_element_type=jnp.float32)
    up = jnp.dot(tokens, up_weight, preferred_element_type=jnp.float32)
    sig = jax.nn.sigmoid(gate)
    hidden = (gate * sig * up).astype(jnp.bfloat16)
    hidden_grad = jnp.dot(cotangent, down_weight.T, preferred_element_type=jnp.float32)
    up_grad = (hidden_grad * gate * sig).astype(jnp.bfloat16)
    gate_grad = (hidden_grad * up * sig * (1.0 + gate * (1.0 - sig))).astype(jnp.bfloat16)
    input_grad = jnp.dot(gate_grad, gate_weight.T, preferred_element_type=jnp.float32)
    input_grad = input_grad + jnp.dot(up_grad, up_weight.T, preferred_element_type=jnp.float32)
    input_grad = input_grad.astype(jnp.bfloat16)

    groups = TOKENS // GROUP
    tok_groups = tokens.reshape(groups, GROUP, D)
    cot_groups = cotangent.reshape(groups, GROUP, D)
    gg_groups = gate_grad.reshape(groups, GROUP, FF)
    ug_groups = up_grad.reshape(groups, GROUP, FF)
    hid_groups = hidden.reshape(groups, GROUP, FF)

    def rounded(value):
        narrow = lax.optimization_barrier(value.astype(jnp.bfloat16))
        return narrow.astype(jnp.float32)

    def add_group(carry, items):
        acc_gate, acc_up, acc_down = carry
        tok_g, cot_g, gg_g, ug_g, hid_g = items
        acc_gate = acc_gate + rounded(jnp.dot(tok_g.T, gg_g, preferred_element_type=jnp.float32))
        acc_up = acc_up + rounded(jnp.dot(tok_g.T, ug_g, preferred_element_type=jnp.float32))
        acc_down = acc_down + rounded(jnp.dot(hid_g.T, cot_g, preferred_element_type=jnp.float32))
        return (acc_gate, acc_up, acc_down), None

    start = (jnp.zeros((D, FF), jnp.float32), jnp.zeros((D, FF), jnp.float32), jnp.zeros((FF, D), jnp.float32))
    totals, unused = lax.scan(add_group, start, (tok_groups, cot_groups, gg_groups, ug_groups, hid_groups))
    grad_gate = (totals[0] / N_DP).astype(jnp.bfloat16)
    grad_up = (totals[1] / N_DP).astype(jnp.bfloat16)
    grad_down = (totals[2] / N_DP).astype(jnp.bfloat16)
    return input_grad, grad_gate, grad_up, grad_down
```

```python
import functools

import jax
import jax.numpy as jnp
from jax import lax
from jax.experimental import pallas as pl
from jax.experimental.pallas import tpu as pltpu
from jax.sharding import PartitionSpec as P

MESH = pl.DeviceIdType.MESH
BF = jnp.bfloat16
F32 = jnp.float32
SHARD = 80
GSH = 48
UNITS = 200
WIDTH = 640
ROWS = 160


def kernel(
    xp_ref, wp_ref, ig_ref, gr_ref,
    tokb, xf, xs, wbuf, fwd, ab, of, ob, pbuf, crecv, psum, xrecv, zsend, zrecv, acc,
    yrecv, ys, nrecv, ns, frecv, ssem, rsem,
):
    dp = lax.axis_index("dp")
    t = lax.axis_index("tensor")
    x, h, c = dp // 4, (dp // 2) % 2, dp % 2
    zl, y = t // 4, t % 4
    q, j = zl // 4, zl % 4

    def dev(x=x, h=h, c=c, q=q, j=j, y=y):
        return ((x * 2 + h) * 2 + c, (q * 4 + j) * 4 + y)

    def up4(v, k):
        return lax.rem(v + k, 4)

    far = [dev(q=up4(q, k)) for k in (1, 2, 3)]
    near = [dev(j=up4(j, k)) for k in (1, 2, 3)]
    ypeer = [dev(y=up4(y, k)) for k in (1, 2, 3)]
    xpeer = [dev(x=up4(x, k)) for k in (1, 2, 3)]
    zpeer = dev(h=1 - h)
    sib = dev(c=1 - c)
    partners = far + near + ypeer + xpeer + [zpeer, sib]

    counter = [0]
    started = []

    def send(src, dst, device):
        i = counter[0]
        counter[0] += 1
        cp = pltpu.make_async_remote_copy(
            src_ref=src, dst_ref=dst, send_sem=ssem.at[i], recv_sem=rsem.at[i],
            device_id=device, device_id_type=MESH,
        )
        cp.start()
        started.append(cp)
        return cp

    barrier = pltpu.get_barrier_semaphore()
    for d in partners:
        pl.semaphore_signal(barrier, inc=1, device_id=d, device_id_type=MESH)

    slot = y * 16 + j * 4 + q
    tokb[slot] = xp_ref[...]
    wbuf[dp] = wp_ref[...]
    of[...] = jnp.zeros_like(of)
    pl.semaphore_wait(barrier, len(partners))

    far_c = [send(tokb.at[slot], tokb.at[slot], far[k]) for k in range(3)]
    xown = [send(wbuf.at[dp], wbuf.at[dp], xpeer[k]) for k in range(3)]
    core_c = [send(wbuf.at[dp], wbuf.at[dp], sib)]
    halves = [pl.ds(0, 80), pl.ds(80, 80)]
    z_c = [send(wbuf.at[dp, r], wbuf.at[dp, r], zpeer) for r in halves]

    for k in range(3):
        xown[k].wait_recv()
        s = (up4(x, 3 - k) * 2 + h) * 2 + c
        core_c.append(send(wbuf.at[s], wbuf.at[s], sib))
    for cp in far_c:
        cp.wait_recv()
    chunk = pl.ds(y * 16 + j * 4, 4)
    near_c = [send(tokb.at[chunk], tokb.at[chunk], near[k]) for k in range(3)]
    for cp in near_c:
        cp.wait_recv()
    chunk = pl.ds(y * 16, 16)
    y_c = [send(tokb.at[chunk], tokb.at[chunk], ypeer[k]) for k in range(3)]

    other = (x * 2 + 1 - h) * 2 + c
    xfw = []
    for i, r in enumerate(halves):
        z_c[i].wait_recv()
        xfw.append([send(wbuf.at[other, r], wbuf.at[other, r], xpeer[k]) for k in range(3)])
        core_c.append(send(wbuf.at[other, r], wbuf.at[other, r], sib))
        if i == 0:
            for cp in y_c:
                cp.wait_recv()
            xf[...] = tokb[...].astype(F32).reshape(64 * SHARD, 128)
            for a in range(2):
                for k in range(2):
                    for b in range(20):
                        v = xf[pl.ds(a * 40 + k * 20 + b, 64, stride=SHARD), :]
                        xs[pl.ds(a * 128 + k * 64, 64), pl.ds(b * 128, 128)] = v.astype(BF)
    for i, r in enumerate(halves):
        for k in range(3):
            xfw[i][k].wait_recv()
            s = (up4(x, 3 - k) * 2 + 1 - h) * 2 + c
            core_c.append(send(wbuf.at[s, r], wbuf.at[s, r], sib))
    for cp in core_c:
        cp.wait_recv()

    fwd[...] = jnp.zeros_like(fwd)

    def forward(i, carry):
        d = pl.ds(pl.multiple_of(i * 640, 640), 640)
        w = wbuf[pl.ds(i * 4, 4)].reshape(640, WIDTH)
        fwd[...] += jnp.dot(xs[:, d], w, preferred_element_type=F32)
        return carry

    lax.fori_loop(0, 4, forward, 0)
    g = fwd[0:128, :]
    gate = g[:, :256]
    upv = pltpu.roll(g, WIDTH - UNITS, 1)[:, :256]
    hg = pltpu.roll(fwd[128:256, :], WIDTH - 2 * UNITS, 1)[:, :256]
    sig = 1.0 / (1.0 + jnp.exp(-gate))
    keep = lax.broadcasted_iota(jnp.int32, (128, 256), 1) < UNITS
    rest = jnp.zeros((128, WIDTH - 256), F32)

    def wide(v, shift):
        v = jnp.concatenate([jnp.where(keep, v, 0.0), rest], axis=1)
        return pltpu.roll(v, shift, 1) if shift else v

    hidden = wide(gate * sig * upv, 2 * UNITS)
    gg = wide(hg * upv * sig * (1.0 + gate * (1.0 - sig)), 0)
    ug = wide(hg * gate * sig, UNITS)
    ab[0:128, :] = (gg + ug).astype(BF)
    ab[128:256, :] = hidden.astype(BF)

    def partial(i, carry):
        d = pl.ds(pl.multiple_of(i * 640, 640), 640)
        p = lax.dot_general(xs[:, d], ab[...], (((0,), (0,)), ((), ())), preferred_element_type=F32)
        p = p.astype(BF)
        for b in range(4):
            pbuf[(b % 2) * 8 + (b // 2) * 4 + i] = p[b * ROWS : (b + 1) * ROWS, :]
        return carry

    lax.fori_loop(0, 4, partial, 0)
    pc = []
    for hh in (1 - h, h):
        src = pl.ds((1 - c) * 8 + hh * 4, 4)
        pc.append(send(pbuf.at[src], crecv.at[pl.ds(hh * 4, 4)], sib))

    for i in range(4):
        w = wbuf[i * 4 : i * 4 + 4].reshape(640, WIDTH)
        tot = lax.dot_general(ab[0:128, :], w, (((1,), (1,)), ((), ())), preferred_element_type=F32)
        for k in range(2):
            for b in range(5):
                of[pl.ds(k * 20 + i * 5 + b, 64, stride=GSH), :] = tot[
                    k * 64 : k * 64 + 64, b * 128 : b * 128 + 128
                ]
    ob[...] = of[...].reshape(64, GSH, 128).astype(BF)
    yg = [
        send(ob.at[pl.ds(up4(y, k + 1) * 16, 16)], yrecv.at[k], ypeer[k]) for k in range(3)
    ]

    px = []
    for n, hh in enumerate((1 - h, h)):
        pc[n].wait_recv()
        for i in range(4):
            a = pbuf[c * 8 + hh * 4 + i].astype(F32) + crecv[hh * 4 + i].astype(F32)
            psum[hh * 4 + i] = a.astype(BF)
        px.append(
            [send(psum.at[hh * 4 + up4(x, k + 1)], xrecv.at[n, k], xpeer[k]) for k in range(3)]
        )
    for n, hh in enumerate((1 - h, h)):
        for cp in px[n]:
            cp.wait_recv()
        a = psum[hh * 4 + x].astype(F32)
        for k in range(3):
            a = a + xrecv[n, k].astype(F32)
        if n == 0:
            zsend[...] = a.astype(BF)
            pz = send(zsend, zrecv, zpeer)
            for cp in yg:
                cp.wait_recv()
            s = ob[pl.ds(y * 16, 16)].astype(F32)
            for k in range(3):
                s = s + yrecv[k].astype(F32)
            ys[...] = s.astype(BF)
            ng = [
                send(ys.at[pl.ds(up4(j, k + 1) * 4, 4)], nrecv.at[k], near[k]) for k in range(3)
            ]
        else:
            acc[...] = a
    for cp in ng:
        cp.wait_recv()
    s = ys[pl.ds(j * 4, 4)].astype(F32)
    for k in range(3):
        s = s + nrecv[k].astype(F32)
    ns[...] = s.astype(BF)
    fg = [send(ns.at[up4(q, k + 1)], frecv.at[k], far[k]) for k in range(3)]
    for cp in fg:
        cp.wait_recv()
    s = ns[q].astype(F32)
    for k in range(3):
        s = s + frecv[k].astype(F32)
    ig_ref[...] = s.astype(BF)
    pz.wait_recv()
    gr_ref[...] = ((acc[...] + zrecv[...].astype(F32)) * (1.0 / 16.0)).astype(BF)
    for cp in started:
        cp.wait_send()


COPIES = 64


def local(tokens, cotangent, gate_weight, up_weight, down_weight):
    xp = jnp.concatenate([tokens, cotangent], axis=0).reshape(SHARD, 128)
    wp = jnp.concatenate(
        [gate_weight, up_weight, down_weight.T, jnp.zeros((ROWS, WIDTH - 3 * UNITS), BF)], axis=1
    )
    vmem = pl.BlockSpec(memory_space=pltpu.VMEM)
    ig, gr = pl.pallas_call(
        kernel,
        name="swiglu_backward",
        out_shape=(
            jax.ShapeDtypeStruct((GSH, 128), BF),
            jax.ShapeDtypeStruct((ROWS, WIDTH), BF),
        ),
        in_specs=[vmem, vmem],
        out_specs=(vmem, vmem),
        scratch_shapes=[
            pltpu.VMEM((64, SHARD, 128), BF),
            pltpu.VMEM((64 * SHARD, 128), F32),
            pltpu.VMEM((256, 2560), BF),
            pltpu.VMEM((16, ROWS, WIDTH), BF),
            pltpu.VMEM((256, WIDTH), F32),
            pltpu.VMEM((256, WIDTH), BF),
            pltpu.VMEM((64 * GSH, 128), F32),
            pltpu.VMEM((64, GSH, 128), BF),
            pltpu.VMEM((16, ROWS, WIDTH), BF),
            pltpu.VMEM((8, ROWS, WIDTH), BF),
            pltpu.VMEM((8, ROWS, WIDTH), BF),
            pltpu.VMEM((2, 3, ROWS, WIDTH), BF),
            pltpu.VMEM((ROWS, WIDTH), BF),
            pltpu.VMEM((ROWS, WIDTH), BF),
            pltpu.VMEM((ROWS, WIDTH), F32),
            pltpu.VMEM((3, 16, GSH, 128), BF),
            pltpu.VMEM((16, GSH, 128), BF),
            pltpu.VMEM((3, 4, GSH, 128), BF),
            pltpu.VMEM((4, GSH, 128), BF),
            pltpu.VMEM((3, GSH, 128), BF),
            pltpu.SemaphoreType.DMA((COPIES,)),
            pltpu.SemaphoreType.DMA((COPIES,)),
        ],
        compiler_params=pltpu.CompilerParams(
            collective_id=0, has_side_effects=True, vmem_limit_bytes=50 * 1024 * 1024
        ),
    )(xp, wp)
    input_grad = ig[:40].reshape(2, 2560)
    return (
        input_grad,
        gr[:, :UNITS],
        gr[:, UNITS : 2 * UNITS],
        gr[:, 2 * UNITS : 3 * UNITS].T,
    )


def solution(mesh):
    placed = (
        P(("dp", "tensor"), None),
        P(("dp", "tensor"), None),
        P("dp", "tensor"),
        P("dp", "tensor"),
        P("tensor", "dp"),
    )
    return jax.shard_map(
        local,
        mesh=mesh,
        in_specs=placed,
        out_specs=(
            P(("dp", "tensor"), None),
            P("dp", "tensor"),
            P("dp", "tensor"),
            P("tensor", "dp"),
        ),
        check_vma=False,
    )
```

```python
import jax
import jax.numpy as jnp
from jax import lax
from jax.experimental import pallas as pl
from jax.experimental.pallas import tpu as pltpu
from jax.sharding import PartitionSpec as P

MESH = pl.DeviceIdType.MESH
BF = jnp.bfloat16
F32 = jnp.float32
SHARD = 80
GROWS = 40
GPAD = 48
UNITS = 100
PACK = 320
WIDTH = 2 * PACK
HALF = 80
COPIES = 128


def kernel(
    xp_ref, wp_ref, ig_ref, gr_ref,
    tokb, xf, xs, wbuf, wz, fwd, ab1, ab2, of, ob, pbuf, crecv, psum, xrecv, zsum, pz,
    yrecv, ys, nrecv, n2recv, fs, rp, rm, sp, sm, ssem, rsem,
):
    dp = lax.axis_index("dp")
    t = lax.axis_index("tensor")
    x, h, c = dp // 4, (dp // 2) % 2, dp % 2
    zl, y = t // 4, t % 4
    z = h * 16 + zl
    q, j = z // 4, z % 4

    def dev(x=x, z=z, c=c, y=y):
        z = lax.rem(z + 32, 32)
        return ((x * 2 + z // 16) * 2 + c, lax.rem(z, 16) * 4 + y)

    def up4(v, k):
        return lax.rem(v + k, 4)

    zp4, zm4, zp1, zm1, zp2, zm2 = [dev(z=z + k) for k in (4, -4, 1, -1, 2, -2)]
    ypeer = [dev(y=up4(y, k)) for k in (1, 2, 3)]
    xpeer = [dev(x=up4(x, k)) for k in (1, 2, 3)]
    sib = dev(c=1 - c)
    partners = [zp4, zm4, zp1, zm1, zp2, zm2] + ypeer + xpeer + [sib]
    turn = 4 - 8 * c
    ahead, behind = dev(z=z + turn), dev(z=z - turn)
    parts = [(ahead, turn, 0), (ahead, turn, 16), (ahead, turn, 32), (behind, -turn, 48), (behind, -turn, 64)]

    counter = [0]
    started = []

    def send(src, dst, device):
        i = counter[0]
        counter[0] += 1
        cp = pltpu.make_async_remote_copy(
            src_ref=src, dst_ref=dst, send_sem=ssem.at[i], recv_sem=rsem.at[i],
            device_id=device, device_id_type=MESH,
        )
        cp.start()
        started.append(cp)
        return cp

    barrier = pltpu.get_barrier_semaphore()
    for d in partners:
        pl.semaphore_signal(barrier, inc=1, device_id=d, device_id_type=MESH)
    base = y * 32 + j * 8

    def at(k):
        return base + lax.rem(q + k + 8, 8)

    tokb[at(0)] = xp_ref[...]
    wbuf[dp] = wp_ref[h]
    fs[...] = jnp.zeros_like(fs)
    pl.semaphore_wait(barrier, len(partners))

    fa = send(tokb.at[at(0)], tokb.at[at(0)], zp4)
    fb = send(tokb.at[at(0)], tokb.at[at(0)], zm4)
    zw = [
        send(wp_ref.at[1 - h, pl.ds(r, 16)], wz.at[0, pl.ds(r, 16)], d) for d, s, r in parts
    ]
    xown = [send(wbuf.at[dp], wbuf.at[dp], xpeer[k]) for k in range(3)]
    core_c = [send(wbuf.at[dp], wbuf.at[dp], sib)]

    def relay(step):
        for i, (d, s, r) in enumerate(parts):
            zw[i].wait_recv()
            rows = pl.ds(r, 16)
            if step < 3:
                dst = wz.at[step, rows]
            else:
                to = lax.rem(z + s + 32, 32) // 16
                dst = wbuf.at[(x * 2 + 1 - to) * 2 + c, rows]
            zw[i] = send(wz.at[step - 1, rows], dst, d)

    for step in (1, 2):
        fa.wait_recv()
        fa = send(tokb.at[at(-step)], tokb.at[at(-step)], zp4)
        fb.wait_recv()
        fb = send(tokb.at[at(step)], tokb.at[at(step)], zm4)
        relay(step)
        if step == 1:
            for k in range(3):
                xown[k].wait_recv()
                s = (up4(x, 3 - k) * 2 + h) * 2 + c
                core_c.append(send(wbuf.at[s], wbuf.at[s], sib))
    fa.wait_recv()
    fa = send(tokb.at[at(-3), pl.ds(0, 48)], tokb.at[at(-3), pl.ds(0, 48)], zp4)
    fb.wait_recv()
    fb = send(tokb.at[at(3), pl.ds(48, 32)], tokb.at[at(3), pl.ds(48, 32)], zm4)
    relay(3)
    fa.wait_recv()
    fb.wait_recv()

    def ysend(residue):
        piece = pl.ds(y * 32 + residue * 8, 8)
        return [send(tokb.at[piece], tokb.at[piece], ypeer[k]) for k in range(3)]

    mine = pl.ds(base, 8)
    low, high = pl.ds(base, 4), pl.ds(base + 4, 4)
    n1 = [send(tokb.at[mine], tokb.at[mine], d) for d in (zp1, zm1)]
    n2 = [send(tokb.at[low], tokb.at[low], zp2), send(tokb.at[high], tokb.at[high], zm2)]
    yc = [ysend(j)]
    n1[0].wait_recv()
    yc.append(ysend(up4(j, 3)))
    n1[1].wait_recv()
    yc.append(ysend(up4(j, 1)))
    for cp in n2:
        cp.wait_recv()
    yc.append(ysend(up4(j, 2)))

    other = (x * 2 + 1 - h) * 2 + c
    for cp in zw:
        cp.wait_recv()
    xfw = [send(wbuf.at[other], wbuf.at[other], xpeer[k]) for k in range(3)]
    core_c.append(send(wbuf.at[other], wbuf.at[other], sib))

    def unpack(yy):
        xf[...] = tokb[pl.ds(yy * 32, 32)].astype(F32).reshape(32 * SHARD, 128)
        for a in range(2):
            for k in range(2):
                rows = pl.ds(pl.multiple_of(a * 256 + k * 128 + yy * 32, 32), 32)
                for b in range(20):
                    v = xf[pl.ds(a * 40 + k * 20 + b, 32, stride=SHARD), :]
                    xs[rows, pl.ds(b * 128, 128)] = v.astype(BF)

    unpack(y)
    for k in range(3):
        xfw[k].wait_recv()
        s = (up4(x, 3 - k) * 2 + 1 - h) * 2 + c
        core_c.append(send(wbuf.at[s], wbuf.at[s], sib))
    for k in (0, 2, 1):
        for piece in yc:
            piece[k].wait_recv()
        unpack(up4(y, 3 - k))
    for cp in core_c:
        cp.wait_recv()

    w = wbuf[...].reshape(1280, WIDTH)
    fwd[...] = jnp.dot(xs[:, 1280:2560], w, preferred_element_type=F32)
    fwd[...] = jnp.dot(xs[:, 0:1280], w, preferred_element_type=F32) + pltpu.roll(
        fwd[...], PACK, 1
    )
    g = fwd[0:256, :256]
    gate = g[:, :128]
    upv = pltpu.roll(g, 256 - UNITS, 1)[:, :128]
    hg = pltpu.roll(fwd[256:512, :384], 384 - 2 * UNITS, 1)[:, :128]
    sig = 1.0 / (1.0 + jnp.exp(-gate))
    keep = lax.broadcasted_iota(jnp.int32, (256, 128), 1) < UNITS
    rest = jnp.zeros((256, WIDTH - 128), F32)

    def wide(v):
        return jnp.concatenate([jnp.where(keep, v, 0.0), rest], axis=1)

    gg = wide(hg * upv * sig * (1.0 + gate * (1.0 - sig)))
    a = gg + pltpu.roll(wide(hg * gate * sig), UNITS, 1)
    ab1[0:256, :] = a.astype(BF)
    ab2[0:256, :] = pltpu.roll(a, PACK, 1).astype(BF)
    a = wide(gate * sig * upv)
    ab1[256:512, :] = pltpu.roll(a, 2 * UNITS, 1).astype(BF)
    ab2[256:512, :] = pltpu.roll(a, PACK + 2 * UNITS, 1).astype(BF)

    tr = (((0,), (0,)), ((), ()))
    for i in range(2):
        p = lax.dot_general(
            xs[:, i * 640 : i * 640 + 640], ab1[...], tr, preferred_element_type=F32
        ) + lax.dot_general(
            xs[:, 1280 + i * 640 : 1920 + i * 640], ab2[...], tr, preferred_element_type=F32
        )
        p = p.astype(BF)
        for b in range(8):
            pbuf[(b % 2) * 8 + ((b // 2) % 2) * 4 + i * 2 + b // 4] = p[b * HALF : (b + 1) * HALF, :]
    pc = []
    for hh in (1 - h, h):
        src = pl.ds((1 - c) * 8 + hh * 4, 4)
        pc.append(send(pbuf.at[src], crecv.at[pl.ds(hh * 4, 4)], sib))

    nt = (((1,), (1,)), ((), ()))
    for e, ab in enumerate((ab1, ab2)):
        for i in range(2):
            w = wbuf[i * 8 : i * 8 + 8].reshape(640, WIDTH)
            tot = lax.dot_general(ab[0:256, :], w, nt, preferred_element_type=F32)
            for k in range(2):
                for b in range(5):
                    of[pl.ds(k * 20 + e * 10 + i * 5 + b, 128, stride=GROWS), :] = tot[
                        k * 128 : k * 128 + 128, b * 128 : b * 128 + 128
                    ]
    ob[...] = of[...].reshape(64, 80, 128).astype(BF)
    yg = [
        send(ob.at[pl.ds(up4(y, k + 1) * 16, 16)], yrecv.at[k], ypeer[k]) for k in range(3)
    ]

    px = []
    for n, hh in enumerate((1 - h, h)):
        pc[n].wait_recv()
        for i in range(4):
            a = pbuf[c * 8 + hh * 4 + i].astype(F32) + crecv[hh * 4 + i].astype(F32)
            psum[hh * 4 + i] = a.astype(BF)
        px.append(
            [send(psum.at[hh * 4 + up4(x, k + 1)], xrecv.at[n, k], xpeer[k]) for k in range(3)]
        )

    def xsum(n, hh):
        for cp in px[n]:
            cp.wait_recv()
        a = psum[hh * 4 + x].astype(F32)
        for k in range(3):
            a = a + xrecv[n, k].astype(F32)
        return (a * (1.0 / 16.0)).astype(BF)

    zsum[...] = xsum(0, 1 - h)
    zw = [send(zsum.at[pl.ds(r, 16)], pz.at[0, pl.ds(r, 16)], d) for d, s, r in parts]

    for cp in yg:
        cp.wait_recv()
    a = ob[pl.ds(y * 16, 16)].astype(F32)
    for k in range(3):
        a = a + yrecv[k].astype(F32)
    ys[...] = a.astype(BF)
    ng = [
        send(ys.at[pl.ds(up4(j, 1) * 4, 4)], nrecv.at[0], zp1),
        send(ys.at[pl.ds(up4(j, 3) * 4, 4)], nrecv.at[1], zm1),
        send(ys.at[pl.ds(up4(j, 2) * 4, 2)], n2recv.at[pl.ds(0, 2)], zp2),
        send(ys.at[pl.ds(up4(j, 2) * 4 + 2, 2)], n2recv.at[pl.ds(2, 2)], zm2),
    ]
    gr_ref[h] = xsum(1, h)
    for cp in ng:
        cp.wait_recv()
    a = ys[pl.ds(j * 4, 4)].astype(F32) + nrecv[0].astype(F32)
    a = a + nrecv[1].astype(F32) + n2recv[...].astype(F32)
    fs[:, 0:GROWS, :] = a.reshape(8, GROWS, 128).astype(BF)

    def own(k):
        return lax.rem(q + k + 8, 8)

    fa = send(fs.at[own(4)], rp.at[0], zp4)
    fb = send(fs.at[own(-3)], rm.at[0], zm4)

    def back(step):
        for i, (d, s, r) in enumerate(parts):
            zw[i].wait_recv()
            rows = pl.ds(r, 16)
            dst = pz.at[step, rows] if step < 3 else pz.at[3, rows]
            zw[i] = send(pz.at[step - 1, rows], dst, d)

    for step in (1, 2, 3):
        fa.wait_recv()
        sp[step - 1] = (rp[step - 1].astype(F32) + fs[own(4 - step)].astype(F32)).astype(BF)
        fa = send(sp.at[step - 1], rp.at[step], zp4)
        fb.wait_recv()
        if step < 3:
            sm[step - 1] = (rm[step - 1].astype(F32) + fs[own(step - 3)].astype(F32)).astype(BF)
            fb = send(sm.at[step - 1], rm.at[step], zm4)
        back(step)
    fa.wait_recv()
    ig_ref[...] = (fs[q].astype(F32) + rm[2].astype(F32) + rp[3].astype(F32)).astype(BF)
    for cp in zw:
        cp.wait_recv()
    gr_ref[1 - h] = pz[3]
    for cp in started:
        cp.wait_send()


def local(tokens, cotangent, gate_weight, up_weight, down_weight):
    xp = jnp.concatenate([tokens, cotangent], axis=0)
    xp = xp.reshape(4, 16, 2, HALF).transpose(0, 2, 1, 3).reshape(SHARD, 128)
    down = down_weight.T
    pad = jnp.zeros((2 * HALF, PACK - 3 * UNITS), BF)
    halves = []
    for i in range(2):
        cut = slice(i * UNITS, (i + 1) * UNITS)
        w = jnp.concatenate([gate_weight[:, cut], up_weight[:, cut], down[:, cut], pad], axis=1)
        halves.append(jnp.concatenate([w[:HALF], w[HALF:]], axis=1))
    wp = jnp.stack(halves)
    vmem = pl.BlockSpec(memory_space=pltpu.VMEM)
    ig, gr = pl.pallas_call(
        kernel,
        name="swiglu_backward",
        out_shape=(
            jax.ShapeDtypeStruct((GPAD, 128), BF),
            jax.ShapeDtypeStruct((2, HALF, WIDTH), BF),
        ),
        in_specs=[vmem, vmem],
        out_specs=(vmem, vmem),
        scratch_shapes=[
            pltpu.VMEM((128, SHARD, 128), BF),
            pltpu.VMEM((32 * SHARD, 128), F32),
            pltpu.VMEM((512, 2560), BF),
            pltpu.VMEM((16, HALF, WIDTH), BF),
            pltpu.VMEM((3, HALF, WIDTH), BF),
            pltpu.VMEM((512, WIDTH), F32),
            pltpu.VMEM((512, WIDTH), BF),
            pltpu.VMEM((512, WIDTH), BF),
            pltpu.VMEM((128 * GROWS, 128), F32),
            pltpu.VMEM((64, 80, 128), BF),
            pltpu.VMEM((16, HALF, WIDTH), BF),
            pltpu.VMEM((8, HALF, WIDTH), BF),
            pltpu.VMEM((8, HALF, WIDTH), BF),
            pltpu.VMEM((2, 3, HALF, WIDTH), BF),
            pltpu.VMEM((HALF, WIDTH), BF),
            pltpu.VMEM((4, HALF, WIDTH), BF),
            pltpu.VMEM((3, 16, 80, 128), BF),
            pltpu.VMEM((16, 80, 128), BF),
            pltpu.VMEM((2, 4, 80, 128), BF),
            pltpu.VMEM((4, 80, 128), BF),
            pltpu.VMEM((8, GPAD, 128), BF),
            pltpu.VMEM((4, GPAD, 128), BF),
            pltpu.VMEM((3, GPAD, 128), BF),
            pltpu.VMEM((3, GPAD, 128), BF),
            pltpu.VMEM((2, GPAD, 128), BF),
            pltpu.SemaphoreType.DMA((COPIES,)),
            pltpu.SemaphoreType.DMA((COPIES,)),
        ],
        compiler_params=pltpu.CompilerParams(
            collective_id=0, has_side_effects=True, vmem_limit_bytes=50 * 1024 * 1024
        ),
    )(xp, wp)
    input_grad = ig[:GROWS].reshape(2, 2, 16, HALF).transpose(0, 2, 1, 3).reshape(2, 2560)
    blocks = [jnp.concatenate([gr[i, :, :PACK], gr[i, :, PACK:]], axis=0) for i in range(2)]
    gate, up, down = (
        jnp.concatenate([b[:, i * UNITS : (i + 1) * UNITS] for b in blocks], axis=1)
        for i in range(3)
    )
    return input_grad, gate, up, down.T


def solution(mesh):
    placed = (
        P(("dp", "tensor"), None),
        P(("dp", "tensor"), None),
        P("dp", "tensor"),
        P("dp", "tensor"),
        P("tensor", "dp"),
    )
    return jax.shard_map(
        local,
        mesh=mesh,
        in_specs=placed,
        out_specs=(
            P(("dp", "tensor"), None),
            P("dp", "tensor"),
            P("dp", "tensor"),
            P("tensor", "dp"),
        ),
        check_vma=False,
    )
```

```python
import jax
import jax.numpy as jnp
from jax import lax
from jax.experimental import pallas as pl
from jax.experimental.pallas import tpu as pltpu
from jax.sharding import PartitionSpec as P

MESH = pl.DeviceIdType.MESH
BF = jnp.bfloat16
F32 = jnp.float32
SHARD = 80
GROWS = 40
GPAD = 48
UNITS = 100
PACK = 320
WIDTH = 2 * PACK
HALF = 80
COPIES = 192


FIRST = [0, 5, 13, 21, 29]
COUNT = [5, 8, 8, 8, 3]
RING = [0, 1, 3, 5, 7]


def kernel(
    xp_ref, wp_ref, ig_ref, gr_ref,
    tokb, xf, xs, wbuf, wz, fwd, ab1, ab2, of, ob, pbuf, crecv, psum, xrecv, zsum, pz,
    yrecv, ys, na, n2, rp, rm, sp, sm, ssem, rsem,
):
    dp = lax.axis_index("dp")
    t = lax.axis_index("tensor")
    x, h, c = dp // 4, (dp // 2) % 2, dp % 2
    zl, y = t // 4, t % 4
    z = h * 16 + zl

    def dev(x=x, z=z, c=c, y=y):
        z = lax.rem(z + 32, 32)
        return ((x * 2 + z // 16) * 2 + c, lax.rem(z, 16) * 4 + y)

    def up4(v, k):
        return lax.rem(v + k, 4)

    zp4, zm4, zp1, zm1, zp2, zm2 = [dev(z=z + k) for k in (4, -4, 1, -1, 2, -2)]
    yp1, yp2, ym1 = [dev(y=up4(y, k)) for k in (1, 2, 3)]
    xpeer = [dev(x=up4(x, k)) for k in (1, 2, 3)]
    sib = dev(c=1 - c)
    partners = [zp4, zm4, zp1, zm1, zp2, zm2, yp1, yp2, ym1] + xpeer + [sib]
    turn = 4 - 8 * c
    ahead, behind = dev(z=z + turn), dev(z=z - turn)
    parts = [(ahead, turn, 0), (ahead, turn, 16), (ahead, turn, 32), (behind, -turn, 48), (behind, -turn, 64)]

    counter = [0]
    started = []

    def send(src, dst, device):
        i = counter[0]
        counter[0] += 1
        cp = pltpu.make_async_remote_copy(
            src_ref=src, dst_ref=dst, send_sem=ssem.at[i], recv_sem=rsem.at[i],
            device_id=device, device_id_type=MESH,
        )
        cp.start()
        started.append(cp)
        return cp

    def arrive(cps):
        for cp in cps:
            cp.wait_recv()

    barrier = pltpu.get_barrier_semaphore()
    for d in partners:
        pl.semaphore_signal(barrier, inc=1, device_id=d, device_id_type=MESH)
    tokb[0] = xp_ref[...]
    wbuf[dp] = wp_ref[h]
    of[...] = jnp.zeros_like(of)
    pl.semaphore_wait(barrier, len(partners))

    def far(step):
        f = FIRST[step]
        to = FIRST[step + 1]
        if step == 0:
            return [send(tokb.at[0], tokb.at[to], zm4), send(tokb.at[0], tokb.at[to + 1], zp4)]
        if step < 3:
            return [send(tokb.at[f], tokb.at[to], zm4), send(tokb.at[f + 1], tokb.at[to + 1], zp4)]
        one, two = pl.ds(0, 48), pl.ds(48, 32)
        return [
            send(tokb.at[f, one], tokb.at[to, one], zm4),
            send(tokb.at[f + 1, two], tokb.at[to, two], zp4),
        ]

    def near(step):
        f = FIRST[step]
        if step in (0, 4):
            out = [send(tokb.at[f], tokb.at[f + 2], zp1), send(tokb.at[f], tokb.at[f + 1], zm1)]
            if step == 0:
                out += [send(tokb.at[0], tokb.at[3], zm2), send(tokb.at[0], tokb.at[4], zp2)]
            return out
        pair = tokb.at[pl.ds(f, 2)]
        return [
            send(pair, tokb.at[pl.ds(f + 4, 2)], zp1),
            send(pair, tokb.at[pl.ds(f + 2, 2)], zm1),
            send(tokb.at[f], tokb.at[f + 6], zm2),
            send(tokb.at[f + 1], tokb.at[f + 7], zp2),
        ]

    def yfirst(step):
        src = tokb.at[pl.ds(FIRST[step], COUNT[step])]
        return [
            send(src, tokb.at[pl.ds(32 + FIRST[step], COUNT[step])], yp1),
            send(src, tokb.at[pl.ds(64 + FIRST[step], COUNT[step])], ym1),
        ]

    def ysecond(step, cps):
        f, n = FIRST[step], COUNT[step]
        k = n // 2
        cps[0].wait_recv()
        out = [send(tokb.at[pl.ds(32 + f, k)], tokb.at[pl.ds(96 + f, k)], yp1)]
        cps[1].wait_recv()
        out.append(send(tokb.at[pl.ds(64 + f + k, n - k)], tokb.at[pl.ds(96 + f + k, n - k)], ym1))
        return out

    zw = []

    def relay(step):
        for i, (d, s, r) in enumerate(parts):
            rows = pl.ds(r, 16)
            if step == 0:
                zw.append(send(wp_ref.at[1 - h, rows], wz.at[0, rows], d))
                continue
            zw[i].wait_recv()
            if step < 3:
                dst = wz.at[step, rows]
            else:
                to = lax.rem(z + s + 32, 32) // 16
                dst = wbuf.at[(x * 2 + 1 - to) * 2 + c, rows]
            zw[i] = send(wz.at[step - 1, rows], dst, d)

    fc = [far(0)]
    nc = [near(0)]
    relay(0)
    xown = [send(wbuf.at[dp], wbuf.at[dp], xpeer[k]) for k in range(3)]
    core_c = [send(wbuf.at[dp], wbuf.at[dp], sib)]
    y1, y2 = [], []
    for step in (1, 2, 3, 4):
        arrive(fc[step - 1])
        if step < 4:
            fc.append(far(step))
        nc.append(near(step))
        arrive(nc[step - 1])
        y1.append(yfirst(step - 1))
        if step < 4:
            relay(step)
        if step == 1:
            for k in range(3):
                xown[k].wait_recv()
                s = (up4(x, 3 - k) * 2 + h) * 2 + c
                core_c.append(send(wbuf.at[s], wbuf.at[s], sib))
        else:
            y2.append(ysecond(step - 2, y1[step - 2]))
    arrive(nc[4])
    y1.append(yfirst(4))
    other = (x * 2 + 1 - h) * 2 + c
    groups = [(pl.ds(0, 48), zw[:3]), (pl.ds(48, 32), zw[3:])]
    xfw = []
    for rows, cps in groups:
        arrive(cps)
        block = wbuf.at[other, rows]
        xfw.append([send(block, block, xpeer[k]) for k in range(3)])
        core_c.append(send(block, block, sib))
    y2.append(ysecond(3, y1[3]))

    def unpack(yy):
        xf[...] = tokb[yy * 32 : yy * 32 + 32].astype(F32).reshape(32 * SHARD, 128)
        for a in range(2):
            for k in range(2):
                row = a * 256 + yy * 64 + k * 32
                for b in range(20):
                    v = xf[pl.ds(a * 40 + k * 20 + b, 32, stride=SHARD), :]
                    xs[row : row + 32, b * 128 : b * 128 + 128] = v.astype(BF)

    y2.append(ysecond(4, y1[4]))
    for i, (rows, cps) in enumerate(groups):
        for k in range(3):
            cps = xfw[i][k]
            cps.wait_recv()
            block = wbuf.at[(up4(x, 3 - k) * 2 + 1 - h) * 2 + c, rows]
            core_c.append(send(block, block, sib))
    unpack(0)
    unpack(1)
    unpack(2)
    for cps in y2:
        arrive(cps)
    unpack(3)
    arrive(core_c)

    w = wbuf[...].reshape(1280, WIDTH)
    fwd[...] = jnp.dot(xs[:, 1280:2560], w, preferred_element_type=F32)
    fwd[...] = jnp.dot(xs[:, 0:1280], w, preferred_element_type=F32) + pltpu.roll(
        fwd[...], PACK, 1
    )
    g = fwd[0:256, :256]
    gate = g[:, :128]
    upv = pltpu.roll(g, 256 - UNITS, 1)[:, :128]
    hg = pltpu.roll(fwd[256:512, :384], 384 - 2 * UNITS, 1)[:, :128]
    sig = 1.0 / (1.0 + jnp.exp(-gate))
    keep = lax.broadcasted_iota(jnp.int32, (256, 128), 1) < UNITS
    rest = jnp.zeros((256, WIDTH - 128), F32)

    def wide(v):
        return jnp.concatenate([jnp.where(keep, v, 0.0), rest], axis=1)

    gg = wide(hg * upv * sig * (1.0 + gate * (1.0 - sig)))
    a = gg + pltpu.roll(wide(hg * gate * sig), UNITS, 1)
    ab1[0:256, :] = a.astype(BF)
    ab2[0:256, :] = pltpu.roll(a, PACK, 1).astype(BF)
    a = wide(gate * sig * upv)
    ab1[256:512, :] = pltpu.roll(a, 2 * UNITS, 1).astype(BF)
    ab2[256:512, :] = pltpu.roll(a, PACK + 2 * UNITS, 1).astype(BF)

    tr = (((0,), (0,)), ((), ()))
    for i in range(2):
        p = lax.dot_general(
            xs[:, i * 640 : i * 640 + 640], ab1[...], tr, preferred_element_type=F32
        ) + lax.dot_general(
            xs[:, 1280 + i * 640 : 1920 + i * 640], ab2[...], tr, preferred_element_type=F32
        )
        p = p.astype(BF)
        for b in range(8):
            pbuf[(b % 2) * 8 + ((b // 2) % 2) * 4 + i * 2 + b // 4] = p[b * HALF : (b + 1) * HALF, :]

    def core(hh):
        src = pl.ds((1 - c) * 8 + hh * 4, 4)
        return send(pbuf.at[src], crecv.at[pl.ds(hh * 4, 4)], sib)

    pc = core(1 - h)

    nt = (((1,), (1,)), ((), ()))
    for e, ab in enumerate((ab1, ab2)):
        for i in range(2):
            w = wbuf[i * 8 : i * 8 + 8].reshape(640, WIDTH)
            tot = lax.dot_general(ab[0:256, :], w, nt, preferred_element_type=F32)
            for yy in range(4):
                for k in range(2):
                    row = yy * 64 + k * 32
                    for b in range(5):
                        at = yy * 32 * GPAD + k * 20 + e * 10 + i * 5 + b
                        of[pl.ds(at, 32, stride=GPAD), :] = tot[row : row + 32, b * 128 : b * 128 + 128]
    ob[...] = of[...].reshape(128, GPAD, 128).astype(BF)

    yg = [None] * 5
    for step in (4, 3, 2, 1, 0):
        f, n = FIRST[step], COUNT[step]
        yg[step] = [
            send(ob.at[pl.ds(32 * (k + 1) + f, n)], yrecv.at[k, pl.ds(f, n)], d)
            for k, d in ((2, yp2), (0, ym1), (1, yp1))
        ]

    def ynear(step):
        f, n, r = FIRST[step], COUNT[step], RING[step]
        arrive(yg[step])
        a = ob[f : f + n].astype(F32)
        for k in range(3):
            a = a + yrecv[k, f : f + n].astype(F32)
        ys[f : f + n] = a.astype(BF)
        if step in (0, 4):
            out = [send(ys.at[f + 1], na.at[1, r], zp1), send(ys.at[f + 2], na.at[0, r], zm1)]
            if step == 0:
                out += [send(ys.at[3], n2.at[0, 0], zp2), send(ys.at[4], n2.at[1, 0], zm2)]
            return out
        return [
            send(ys.at[pl.ds(f + 2, 2)], na.at[1, pl.ds(r, 2)], zp1),
            send(ys.at[pl.ds(f + 4, 2)], na.at[0, pl.ds(r, 2)], zm1),
            send(ys.at[f + 6], n2.at[0, step], zp2),
            send(ys.at[f + 7], n2.at[1, step], zm2),
        ]

    def ringsum(step, k):
        f, r = FIRST[step] + k, RING[step] + k
        a = ys[f].astype(F32) + na[0, r].astype(F32) + na[1, r].astype(F32)
        if step < 4:
            a = a + n2[k, step].astype(F32)
        if step == 0:
            a = a + n2[1, 0].astype(F32)
        return a

    def coresum(hh):
        for i in range(4):
            a = pbuf[c * 8 + hh * 4 + i].astype(F32) + crecv[hh * 4 + i].astype(F32)
            psum[hh * 4 + i] = a.astype(BF)

    def xsend(n, hh):
        return [send(psum.at[hh * 4 + up4(x, k + 1)], xrecv.at[n, k], xpeer[k]) for k in range(3)]

    def xsum(n, hh, cps):
        arrive(cps)
        a = psum[hh * 4 + x].astype(F32)
        for k in range(3):
            a = a + xrecv[n, k].astype(F32)
        return (a * (1.0 / 16.0)).astype(BF)

    def back(step):
        for i, (d, s, r) in enumerate(parts):
            rows = pl.ds(r, 16)
            if step == 0:
                zw[i] = send(zsum.at[rows], pz.at[0, rows], d)
            else:
                zw[i].wait_recv()
                zw[i] = send(pz.at[step - 1, rows], pz.at[step, rows], d)

    def ringstep(step, plus, minus):
        arrive(ngc[step])
        if step == 4:
            sp[3] = ringsum(4, 0).astype(BF)
            return send(sp.at[3], rp.at[3], zp4), None
        plus.wait_recv()
        sp[step - 1] = (rp[step].astype(F32) + ringsum(step, 0)).astype(BF)
        plus = send(sp.at[step - 1], rp.at[step - 1], zp4)
        a = ringsum(step, 1)
        if step < 3:
            minus.wait_recv()
            a = a + rm[step].astype(F32)
        sm[step - 1] = a.astype(BF)
        minus = send(sm.at[step - 1], rm.at[step - 1], zm4)
        return plus, minus

    ngc = [None] * 5
    pc.wait_recv()
    pc = core(h)
    coresum(1 - h)
    px0 = xsend(0, 1 - h)
    ngc[4] = ynear(4)
    ngc[3] = ynear(3)
    plus, minus = ringstep(4, None, None)
    zsum[...] = xsum(0, 1 - h, px0)
    back(0)
    pc.wait_recv()
    coresum(h)
    px1 = xsend(1, h)
    ngc[2] = ynear(2)
    plus, minus = ringstep(3, plus, minus)
    ngc[1] = ynear(1)
    back(1)
    plus, minus = ringstep(2, plus, minus)
    ngc[0] = ynear(0)
    back(2)
    gr_ref[h] = xsum(1, h, px1)
    plus, minus = ringstep(1, plus, minus)
    back(3)
    arrive(ngc[0])
    plus.wait_recv()
    minus.wait_recv()
    ig_ref[...] = (ringsum(0, 0) + rp[0].astype(F32) + rm[0].astype(F32)).astype(BF)
    arrive(zw)
    gr_ref[1 - h] = pz[3]
    for cp in started:
        cp.wait_send()


def local(tokens, cotangent, gate_weight, up_weight, down_weight):
    xp = jnp.concatenate([tokens, cotangent], axis=0)
    xp = xp.reshape(4, 16, 2, HALF).transpose(0, 2, 1, 3).reshape(SHARD, 128)
    down = down_weight.T
    pad = jnp.zeros((2 * HALF, PACK - 3 * UNITS), BF)
    halves = []
    for i in range(2):
        cut = slice(i * UNITS, (i + 1) * UNITS)
        w = jnp.concatenate([gate_weight[:, cut], up_weight[:, cut], down[:, cut], pad], axis=1)
        halves.append(jnp.concatenate([w[:HALF], w[HALF:]], axis=1))
    wp = jnp.stack(halves)
    vmem = pl.BlockSpec(memory_space=pltpu.VMEM)
    ig, gr = pl.pallas_call(
        kernel,
        name="swiglu_backward",
        out_shape=(
            jax.ShapeDtypeStruct((GPAD, 128), BF),
            jax.ShapeDtypeStruct((2, HALF, WIDTH), BF),
        ),
        in_specs=[vmem, vmem],
        out_specs=(vmem, vmem),
        scratch_shapes=[
            pltpu.VMEM((128, SHARD, 128), BF),
            pltpu.VMEM((32 * SHARD, 128), F32),
            pltpu.VMEM((512, 2560), BF),
            pltpu.VMEM((16, HALF, WIDTH), BF),
            pltpu.VMEM((3, HALF, WIDTH), BF),
            pltpu.VMEM((512, WIDTH), F32),
            pltpu.VMEM((512, WIDTH), BF),
            pltpu.VMEM((512, WIDTH), BF),
            pltpu.VMEM((128 * GPAD, 128), F32),
            pltpu.VMEM((128, GPAD, 128), BF),
            pltpu.VMEM((16, HALF, WIDTH), BF),
            pltpu.VMEM((8, HALF, WIDTH), BF),
            pltpu.VMEM((8, HALF, WIDTH), BF),
            pltpu.VMEM((2, 3, HALF, WIDTH), BF),
            pltpu.VMEM((HALF, WIDTH), BF),
            pltpu.VMEM((4, HALF, WIDTH), BF),
            pltpu.VMEM((3, 32, GPAD, 128), BF),
            pltpu.VMEM((32, GPAD, 128), BF),
            pltpu.VMEM((2, 8, GPAD, 128), BF),
            pltpu.VMEM((2, 4, GPAD, 128), BF),
            pltpu.VMEM((4, GPAD, 128), BF),
            pltpu.VMEM((3, GPAD, 128), BF),
            pltpu.VMEM((4, GPAD, 128), BF),
            pltpu.VMEM((3, GPAD, 128), BF),
            pltpu.SemaphoreType.DMA((COPIES,)),
            pltpu.SemaphoreType.DMA((COPIES,)),
        ],
        compiler_params=pltpu.CompilerParams(
            collective_id=0, has_side_effects=True, vmem_limit_bytes=50 * 1024 * 1024
        ),
    )(xp, wp)
    input_grad = ig[:GROWS].reshape(2, 2, 16, HALF).transpose(0, 2, 1, 3).reshape(2, 2560)
    blocks = [jnp.concatenate([gr[i, :, :PACK], gr[i, :, PACK:]], axis=0) for i in range(2)]
    gate, up, down = (
        jnp.concatenate([b[:, i * UNITS : (i + 1) * UNITS] for b in blocks], axis=1)
        for i in range(3)
    )
    return input_grad, gate, up, down.T


def solution(mesh):
    placed = (
        P(("dp", "tensor"), None),
        P(("dp", "tensor"), None),
        P("dp", "tensor"),
        P("dp", "tensor"),
        P("tensor", "dp"),
    )
    return jax.shard_map(
        local,
        mesh=mesh,
        in_specs=placed,
        out_specs=(
            P(("dp", "tensor"), None),
            P("dp", "tensor"),
            P("dp", "tensor"),
            P("tensor", "dp"),
        ),
        check_vma=False,
    )
```

```python
import jax
import jax.numpy as jnp
from jax import lax
from jax.experimental import pallas as pl
from jax.experimental.pallas import tpu as pltpu
from jax.sharding import PartitionSpec as P

MESH = pl.DeviceIdType.MESH
BF = jnp.bfloat16
F32 = jnp.float32
SHARD = 80
GROWS = 40
GPAD = 48
UNITS = 100
PACK = 320
WIDTH = 2 * PACK
HALF = 80
COPIES = 192


FIRST = [0, 5, 13, 21, 29]
COUNT = [5, 8, 8, 8, 3]
RING = [0, 1, 3, 5, 7]


def kernel(
    xp_ref, wp_ref, ig_ref, gr_ref,
    tokb, xf, xs, wbuf, wz, fwd, ab1, ab2, of, ob, pbuf, crecv, psum, xrecv, zsum, pz,
    yrecv, ys, na, n2, rp, rm, sp, sm, ssem, rsem,
):
    dp = lax.axis_index("dp")
    t = lax.axis_index("tensor")
    x, h, c = dp // 4, (dp // 2) % 2, dp % 2
    zl, y = t // 4, t % 4
    z = h * 16 + zl

    def dev(x=x, z=z, c=c, y=y):
        z = lax.rem(z + 32, 32)
        return ((x * 2 + z // 16) * 2 + c, lax.rem(z, 16) * 4 + y)

    def up4(v, k):
        return lax.rem(v + k, 4)

    zp4, zm4, zp1, zm1, zp2, zm2 = [dev(z=z + k) for k in (4, -4, 1, -1, 2, -2)]
    yp1, yp2, ym1 = [dev(y=up4(y, k)) for k in (1, 2, 3)]
    xpeer = [dev(x=up4(x, k)) for k in (1, 2, 3)]
    sib = dev(c=1 - c)
    partners = [zp4, zm4, zp1, zm1, zp2, zm2, yp1, yp2, ym1] + xpeer + [sib]
    turn = 4 - 8 * c
    ahead, behind = dev(z=z + turn), dev(z=z - turn)
    parts = [(ahead, turn, 0), (ahead, turn, 16), (ahead, turn, 32), (behind, -turn, 48), (behind, -turn, 64)]

    counter = [0]
    started = []

    def send(src, dst, device):
        i = counter[0]
        counter[0] += 1
        cp = pltpu.make_async_remote_copy(
            src_ref=src, dst_ref=dst, send_sem=ssem.at[i], recv_sem=rsem.at[i],
            device_id=device, device_id_type=MESH,
        )
        cp.start()
        started.append(cp)
        return cp

    def arrive(cps):
        for cp in cps:
            cp.wait_recv()

    barrier = pltpu.get_barrier_semaphore()
    for d in partners:
        pl.semaphore_signal(barrier, inc=1, device_id=d, device_id_type=MESH)
    tokb[0] = xp_ref[...]
    wbuf[dp] = wp_ref[h]
    of[...] = jnp.zeros_like(of)
    pl.semaphore_wait(barrier, len(partners))

    def far(step):
        f = FIRST[step]
        to = FIRST[step + 1]
        if step == 0:
            return [send(tokb.at[0], tokb.at[to], zm4), send(tokb.at[0], tokb.at[to + 1], zp4)]
        if step < 3:
            return [send(tokb.at[f], tokb.at[to], zm4), send(tokb.at[f + 1], tokb.at[to + 1], zp4)]
        one, two = pl.ds(0, 48), pl.ds(48, 32)
        return [
            send(tokb.at[f, one], tokb.at[to, one], zm4),
            send(tokb.at[f + 1, two], tokb.at[to, two], zp4),
        ]

    def near(step):
        f = FIRST[step]
        if step in (0, 4):
            out = [send(tokb.at[f], tokb.at[f + 2], zp1), send(tokb.at[f], tokb.at[f + 1], zm1)]
            if step == 0:
                out += [send(tokb.at[0], tokb.at[3], zm2), send(tokb.at[0], tokb.at[4], zp2)]
            return out
        pair = tokb.at[pl.ds(f, 2)]
        return [
            send(pair, tokb.at[pl.ds(f + 4, 2)], zp1),
            send(pair, tokb.at[pl.ds(f + 2, 2)], zm1),
            send(tokb.at[f], tokb.at[f + 6], zm2),
            send(tokb.at[f + 1], tokb.at[f + 7], zp2),
        ]

    def yfirst(step):
        src = tokb.at[pl.ds(FIRST[step], COUNT[step])]
        return [
            send(src, tokb.at[pl.ds(32 + FIRST[step], COUNT[step])], yp1),
            send(src, tokb.at[pl.ds(64 + FIRST[step], COUNT[step])], ym1),
        ]

    def ysecond(step, cps):
        f, n = FIRST[step], COUNT[step]
        k = n // 2
        cps[0].wait_recv()
        out = [send(tokb.at[pl.ds(32 + f, k)], tokb.at[pl.ds(96 + f, k)], yp1)]
        cps[1].wait_recv()
        out.append(send(tokb.at[pl.ds(64 + f + k, n - k)], tokb.at[pl.ds(96 + f + k, n - k)], ym1))
        return out

    zw = []

    def relay(step):
        for i, (d, s, r) in enumerate(parts):
            rows = pl.ds(r, 16)
            if step == 0:
                zw.append(send(wp_ref.at[1 - h, rows], wz.at[0, rows], d))
                continue
            zw[i].wait_recv()
            if step < 3:
                dst = wz.at[step, rows]
            else:
                to = lax.rem(z + s + 32, 32) // 16
                dst = wbuf.at[(x * 2 + 1 - to) * 2 + c, rows]
            zw[i] = send(wz.at[step - 1, rows], dst, d)

    fc = [far(0)]
    nc = [near(0)]
    relay(0)
    xown = [send(wbuf.at[dp], wbuf.at[dp], xpeer[k]) for k in range(3)]
    core_c = [send(wbuf.at[dp], wbuf.at[dp], sib)]
    y1, y2 = [], []
    for step in (1, 2, 3, 4):
        arrive(fc[step - 1])
        if step < 4:
            fc.append(far(step))
        nc.append(near(step))
        arrive(nc[step - 1])
        y1.append(yfirst(step - 1))
        if step < 4:
            relay(step)
        if step == 1:
            for k in range(3):
                xown[k].wait_recv()
                s = (up4(x, 3 - k) * 2 + h) * 2 + c
                core_c.append(send(wbuf.at[s], wbuf.at[s], sib))
        else:
            y2.append(ysecond(step - 2, y1[step - 2]))
    arrive(nc[4])
    y1.append(yfirst(4))
    other = (x * 2 + 1 - h) * 2 + c
    groups = [(pl.ds(0, 48), zw[:3]), (pl.ds(48, 32), zw[3:])]
    xfw = []
    for rows, cps in groups:
        arrive(cps)
        block = wbuf.at[other, rows]
        xfw.append([send(block, block, xpeer[k]) for k in range(3)])
        core_c.append(send(block, block, sib))
    y2.append(ysecond(3, y1[3]))

    def unpack(yy):
        xf[...] = tokb[yy * 32 : yy * 32 + 32].astype(F32).reshape(32 * SHARD, 128)
        for a in range(2):
            for k in range(2):
                row = a * 256 + yy * 64 + k * 32
                for b in range(20):
                    v = xf[pl.ds(a * 40 + k * 20 + b, 32, stride=SHARD), :]
                    xs[row : row + 32, b * 128 : b * 128 + 128] = v.astype(BF)

    y2.append(ysecond(4, y1[4]))
    for i, (rows, cps) in enumerate(groups):
        for k in range(3):
            cps = xfw[i][k]
            cps.wait_recv()
            block = wbuf.at[(up4(x, 3 - k) * 2 + 1 - h) * 2 + c, rows]
            core_c.append(send(block, block, sib))
    unpack(0)
    unpack(1)
    unpack(2)
    for cps in y2:
        arrive(cps)
    unpack(3)
    arrive(core_c)

    w = wbuf[...].reshape(1280, WIDTH)
    fwd[...] = jnp.dot(xs[:, 1280:2560], w, preferred_element_type=F32)
    fwd[...] = jnp.dot(xs[:, 0:1280], w, preferred_element_type=F32) + pltpu.roll(
        fwd[...], PACK, 1
    )
    g = fwd[0:256, :256]
    gate = g[:, :128]
    upv = pltpu.roll(g, 256 - UNITS, 1)[:, :128]
    hg = pltpu.roll(fwd[256:512, :384], 384 - 2 * UNITS, 1)[:, :128]
    sig = 1.0 / (1.0 + jnp.exp(-gate))
    keep = lax.broadcasted_iota(jnp.int32, (256, 128), 1) < UNITS
    rest = jnp.zeros((256, WIDTH - 128), F32)

    def wide(v):
        return jnp.concatenate([jnp.where(keep, v, 0.0), rest], axis=1)

    gg = wide(hg * upv * sig * (1.0 + gate * (1.0 - sig)))
    a = gg + pltpu.roll(wide(hg * gate * sig), UNITS, 1)
    ab1[0:256, :] = a.astype(BF)
    ab2[0:256, :] = pltpu.roll(a, PACK, 1).astype(BF)
    a = wide(gate * sig * upv)
    ab1[256:512, :] = pltpu.roll(a, 2 * UNITS, 1).astype(BF)
    ab2[256:512, :] = pltpu.roll(a, PACK + 2 * UNITS, 1).astype(BF)

    nt = (((1,), (1,)), ((), ()))
    for e, ab in enumerate((ab1, ab2)):
        for i in range(2):
            w = wbuf[i * 8 : i * 8 + 8].reshape(640, WIDTH)
            tot = lax.dot_general(ab[0:256, :], w, nt, preferred_element_type=F32)
            for yy in range(4):
                for k in range(2):
                    row = yy * 64 + k * 32
                    for b in range(5):
                        at = yy * 32 * GPAD + k * 20 + e * 10 + i * 5 + b
                        of[pl.ds(at, 32, stride=GPAD), :] = tot[row : row + 32, b * 128 : b * 128 + 128]
    ob[...] = of[...].reshape(128, GPAD, 128).astype(BF)

    yg = [None] * 5
    for step in (4, 3, 2, 1, 0):
        f, n = FIRST[step], COUNT[step]
        yg[step] = [
            send(ob.at[pl.ds(32 * (k + 1) + f, n)], yrecv.at[k, pl.ds(f, n)], d)
            for k, d in ((2, yp2), (0, ym1), (1, yp1))
        ]

    tr = (((0,), (0,)), ((), ()))
    for i in range(2):
        p = lax.dot_general(
            xs[:, i * 640 : i * 640 + 640], ab1[...], tr, preferred_element_type=F32
        ) + lax.dot_general(
            xs[:, 1280 + i * 640 : 1920 + i * 640], ab2[...], tr, preferred_element_type=F32
        )
        p = p.astype(BF)
        for b in range(8):
            pbuf[(b % 2) * 8 + ((b // 2) % 2) * 4 + i * 2 + b // 4] = p[b * HALF : (b + 1) * HALF, :]

    def core(hh):
        src = pl.ds((1 - c) * 8 + hh * 4, 4)
        return send(pbuf.at[src], crecv.at[pl.ds(hh * 4, 4)], sib)

    pc = core(1 - h)

    def ynear(step):
        f, n, r = FIRST[step], COUNT[step], RING[step]
        arrive(yg[step])
        a = ob[f : f + n].astype(F32)
        for k in range(3):
            a = a + yrecv[k, f : f + n].astype(F32)
        ys[f : f + n] = a.astype(BF)
        if step in (0, 4):
            out = [send(ys.at[f + 1], na.at[1, r], zp1), send(ys.at[f + 2], na.at[0, r], zm1)]
            if step == 0:
                out += [send(ys.at[3], n2.at[0, 0], zp2), send(ys.at[4], n2.at[1, 0], zm2)]
            return out
        return [
            send(ys.at[pl.ds(f + 2, 2)], na.at[1, pl.ds(r, 2)], zp1),
            send(ys.at[pl.ds(f + 4, 2)], na.at[0, pl.ds(r, 2)], zm1),
            send(ys.at[f + 6], n2.at[0, step], zp2),
            send(ys.at[f + 7], n2.at[1, step], zm2),
        ]

    def ringsum(step, k):
        f, r = FIRST[step] + k, RING[step] + k
        a = ys[f].astype(F32) + na[0, r].astype(F32) + na[1, r].astype(F32)
        if step < 4:
            a = a + n2[k, step].astype(F32)
        if step == 0:
            a = a + n2[1, 0].astype(F32)
        return a

    def coresum(hh):
        for i in range(4):
            a = pbuf[c * 8 + hh * 4 + i].astype(F32) + crecv[hh * 4 + i].astype(F32)
            psum[hh * 4 + i] = a.astype(BF)

    def xsend(n, hh):
        return [send(psum.at[hh * 4 + up4(x, k + 1)], xrecv.at[n, k], xpeer[k]) for k in range(3)]

    def xsum(n, hh, cps):
        arrive(cps)
        a = psum[hh * 4 + x].astype(F32)
        for k in range(3):
            a = a + xrecv[n, k].astype(F32)
        return (a * (1.0 / 16.0)).astype(BF)

    def back(step):
        for i, (d, s, r) in enumerate(parts):
            rows = pl.ds(r, 16)
            if step == 0:
                zw[i] = send(zsum.at[rows], pz.at[0, rows], d)
            else:
                zw[i].wait_recv()
                zw[i] = send(pz.at[step - 1, rows], pz.at[step, rows], d)

    def ringstep(step, plus, minus):
        arrive(ngc[step])
        if step == 4:
            sp[3] = ringsum(4, 0).astype(BF)
            return send(sp.at[3], rp.at[3], zp4), None
        plus.wait_recv()
        sp[step - 1] = (rp[step].astype(F32) + ringsum(step, 0)).astype(BF)
        plus = send(sp.at[step - 1], rp.at[step - 1], zp4)
        a = ringsum(step, 1)
        if step < 3:
            minus.wait_recv()
            a = a + rm[step].astype(F32)
        sm[step - 1] = a.astype(BF)
        minus = send(sm.at[step - 1], rm.at[step - 1], zm4)
        return plus, minus

    ngc = [None] * 5
    pc.wait_recv()
    pc = core(h)
    coresum(1 - h)
    px0 = xsend(0, 1 - h)
    ngc[4] = ynear(4)
    ngc[3] = ynear(3)
    plus, minus = ringstep(4, None, None)
    zsum[...] = xsum(0, 1 - h, px0)
    back(0)
    pc.wait_recv()
    coresum(h)
    px1 = xsend(1, h)
    ngc[2] = ynear(2)
    plus, minus = ringstep(3, plus, minus)
    ngc[1] = ynear(1)
    back(1)
    plus, minus = ringstep(2, plus, minus)
    ngc[0] = ynear(0)
    back(2)
    gr_ref[h] = xsum(1, h, px1)
    plus, minus = ringstep(1, plus, minus)
    back(3)
    arrive(ngc[0])
    plus.wait_recv()
    minus.wait_recv()
    ig_ref[...] = (ringsum(0, 0) + rp[0].astype(F32) + rm[0].astype(F32)).astype(BF)
    arrive(zw)
    gr_ref[1 - h] = pz[3]
    for cp in started:
        cp.wait_send()


def local(tokens, cotangent, gate_weight, up_weight, down_weight):
    xp = jnp.concatenate([tokens, cotangent], axis=0)
    xp = xp.reshape(4, 16, 2, HALF).transpose(0, 2, 1, 3).reshape(SHARD, 128)
    down = down_weight.T
    pad = jnp.zeros((2 * HALF, PACK - 3 * UNITS), BF)
    halves = []
    for i in range(2):
        cut = slice(i * UNITS, (i + 1) * UNITS)
        w = jnp.concatenate([gate_weight[:, cut], up_weight[:, cut], down[:, cut], pad], axis=1)
        halves.append(jnp.concatenate([w[:HALF], w[HALF:]], axis=1))
    wp = jnp.stack(halves)
    vmem = pl.BlockSpec(memory_space=pltpu.VMEM)
    ig, gr = pl.pallas_call(
        kernel,
        name="swiglu_backward",
        out_shape=(
            jax.ShapeDtypeStruct((GPAD, 128), BF),
            jax.ShapeDtypeStruct((2, HALF, WIDTH), BF),
        ),
        in_specs=[vmem, vmem],
        out_specs=(vmem, vmem),
        scratch_shapes=[
            pltpu.VMEM((128, SHARD, 128), BF),
            pltpu.VMEM((32 * SHARD, 128), F32),
            pltpu.VMEM((512, 2560), BF),
            pltpu.VMEM((16, HALF, WIDTH), BF),
            pltpu.VMEM((3, HALF, WIDTH), BF),
            pltpu.VMEM((512, WIDTH), F32),
            pltpu.VMEM((512, WIDTH), BF),
            pltpu.VMEM((512, WIDTH), BF),
            pltpu.VMEM((128 * GPAD, 128), F32),
            pltpu.VMEM((128, GPAD, 128), BF),
            pltpu.VMEM((16, HALF, WIDTH), BF),
            pltpu.VMEM((8, HALF, WIDTH), BF),
            pltpu.VMEM((8, HALF, WIDTH), BF),
            pltpu.VMEM((2, 3, HALF, WIDTH), BF),
            pltpu.VMEM((HALF, WIDTH), BF),
            pltpu.VMEM((4, HALF, WIDTH), BF),
            pltpu.VMEM((3, 32, GPAD, 128), BF),
            pltpu.VMEM((32, GPAD, 128), BF),
            pltpu.VMEM((2, 8, GPAD, 128), BF),
            pltpu.VMEM((2, 4, GPAD, 128), BF),
            pltpu.VMEM((4, GPAD, 128), BF),
            pltpu.VMEM((3, GPAD, 128), BF),
            pltpu.VMEM((4, GPAD, 128), BF),
            pltpu.VMEM((3, GPAD, 128), BF),
            pltpu.SemaphoreType.DMA((COPIES,)),
            pltpu.SemaphoreType.DMA((COPIES,)),
        ],
        compiler_params=pltpu.CompilerParams(
            collective_id=0, has_side_effects=True, vmem_limit_bytes=50 * 1024 * 1024
        ),
    )(xp, wp)
    input_grad = ig[:GROWS].reshape(2, 2, 16, HALF).transpose(0, 2, 1, 3).reshape(2, 2560)
    blocks = [jnp.concatenate([gr[i, :, :PACK], gr[i, :, PACK:]], axis=0) for i in range(2)]
    gate, up, down = (
        jnp.concatenate([b[:, i * UNITS : (i + 1) * UNITS] for b in blocks], axis=1)
        for i in range(3)
    )
    return input_grad, gate, up, down.T


def solution(mesh):
    placed = (
        P(("dp", "tensor"), None),
        P(("dp", "tensor"), None),
        P("dp", "tensor"),
        P("dp", "tensor"),
        P("tensor", "dp"),
    )
    return jax.shard_map(
        local,
        mesh=mesh,
        in_specs=placed,
        out_specs=(
            P(("dp", "tensor"), None),
            P("dp", "tensor"),
            P("dp", "tensor"),
            P("tensor", "dp"),
        ),
        check_vma=False,
    )
```
